32 devices in a mesh: seq: 16 (over z, x, core), head: 2 (over y).
Axes of the slice: x: 2, y: 2, z: 4, core: 2. Of those that a mesh axis runs over, the one named last changes fastest.
Arguments:
- queries: bfloat16 [4096, 512], P('seq', 'head'), may hold values from -6 to 6
- key_rows: bfloat16 [4096, 512], P('seq', 'head'), may hold values from -6 to 6
- value_rows: bfloat16 [4096, 1024], P('seq', 'head'), may hold values from -6 to 6
- log_decay: float32 [2, 4096], P('head', 'seq'), may hold values from -1.5 to 0, as said below
- upstream: bfloat16 [4096, 1024], P(('seq', 'head')), may hold values from -6 to 6
- norm_gain: float32 [2, 512], P('head'), may hold values from 0.25 to 1.75
Outputs:
- query_grad: bfloat16 [4096, 512], P('seq', 'head')
- key_grad: bfloat16 [4096, 512], P('seq', 'head')
- value_grad: bfloat16 [4096, 1024], P('seq', 'head')
- gain_grad: float32 [2, 512], P('head')
- bias_grad: float32 [2, 512], P('head')
The draws below stay inside these ranges and needn't reach their ends.
Inputs may be any that keep to these rules, and one draw needn't show every extreme that they name: log_decay is never positive.
All inputs are finite; a program needn't handle non-finite values.
Results may differ from the reference program's by a relative error of at most 0.0067.
Values may be sent and summed in bfloat16 or wider, within the bound.
A program may use at most 64 MiB of HBM per device.

```python
import math
import jax
import jax.numpy as jnp
from jax import lax

DK = 256
DV = 512
HEAD_TOTAL = 2
TOKEN_TOTAL = 4096
N_SEQ = 16


def draw_log_decay(key, part):
    random_subkeys = jax.random.split(jax.random.fold_in(key, 11), 6)
    slow_share = 0.5
    slow_heads = jax.random.uniform(random_subkeys[0], (HEAD_TOTAL, 1)) < slow_share
    fast_rates = jnp.exp(jax.random.uniform(random_subkeys[1], (HEAD_TOTAL, 1), minval=math.log(1.0 / 50.0), maxval=math.log(1.0 / 30.0)))
    slow_rates = jnp.exp(jax.random.uniform(random_subkeys[2], (HEAD_TOTAL, 1), minval=math.log(0.2), maxval=math.log(0.6))) / TOKEN_TOTAL
    baseline_rates = jnp.where(slow_heads, slow_rates, fast_rates)
    jaggedness = jnp.exp(jax.random.uniform(random_subkeys[3], (HEAD_TOTAL, TOKEN_TOTAL), minval=math.log(0.7), maxval=math.log(1.4)))
    spike_position = jax.random.randint(random_subkeys[4], (HEAD_TOTAL, 2, 1), 0, TOKEN_TOTAL)
    token_spots = jnp.arange(TOKEN_TOTAL)
    spike_struck = jnp.sum((token_spots[None, None, :] == spike_position).astype(jnp.float32), axis=1)
    loss_fraction = jax.random.uniform(random_subkeys[5], (HEAD_TOTAL, TOKEN_TOTAL), minval=0.2, maxval=0.5)
    return (-baseline_rates * jaggedness + spike_struck * jnp.log1p(-loss_fraction)).astype(jnp.float32)


def draw_upstream(key, part):
    random_subkeys = jax.random.split(jax.random.fold_in(key, 23), 3)
    token_spots = jnp.arange(TOKEN_TOTAL).astype(jnp.float32)[:, None] / TOKEN_TOTAL
    ramp_up = 0.5 + token_spots
    values = jnp.clip(jax.random.normal(random_subkeys[2], (TOKEN_TOTAL, HEAD_TOTAL * DV)), -4.0, 4.0) * ramp_up
    return values.astype(jnp.bfloat16)


def shard_levels(stream_key, dims, pieces, least, largest):
    def one(axis_at, blocks):
        heights = jax.random.uniform(jax.random.fold_in(jax.random.fold_in(stream_key, 6), axis_at), (blocks,), jnp.float32, least / len(pieces), largest / len(pieces))
        return jnp.repeat(jnp.exp(heights), dims[axis_at] // blocks).reshape((-1,) + (1,) * (len(dims) - axis_at - 1))

    factor_of = one(*pieces[0])
    for cut in pieces[1:]:
        factor_of = factor_of * one(*cut)
    return factor_of


def noise(key, shape, width, most, pieces=(), held_as=jnp.bfloat16):
    level = shard_levels(key, shape, pieces, -0.22, 0.18) if pieces else 1.0
    values = jax.random.normal(key, shape, jnp.float32) * width * level
    return jnp.minimum(jnp.maximum(values, -most), most).astype(held_as)


def setup_inputs(seed: int = 0) -> dict:
    streams_of = jax.random.split(jax.random.key(seed), 7)
    return {
        "queries": noise(streams_of[0], (TOKEN_TOTAL, HEAD_TOTAL * DK), 1.0, 6.0, ((0, 16), (1, 2))),
        "key_rows": noise(streams_of[1], (TOKEN_TOTAL, HEAD_TOTAL * DK), 1.0, 6.0, ((0, 16), (1, 2))),
        "value_rows": noise(streams_of[2], (TOKEN_TOTAL, HEAD_TOTAL * DV), 1.0, 6.0, ((0, 16), (1, 2))),
        "log_decay": draw_log_decay(jax.random.fold_in(streams_of[6], 71), 0),
        "upstream": draw_upstream(jax.random.fold_in(streams_of[6], 71), 0),
        "norm_gain": jnp.clip(1.0 + 0.15 * jax.random.normal(streams_of[5], (HEAD_TOTAL, DV), jnp.float32), 0.25, 1.75),
    }


norm_eps = 1e-05

def decay_matrix(running):
    length = running.shape[0]
    positions = jnp.arange(length)
    lower = positions[:, None] >= positions[None, :]
    spread = jnp.where(lower, running[:, None] - running[None, :], 0.0)
    return jnp.where(lower, jnp.exp(spread), 0.0)

def block_terms(query_rows, key_rows, value_rows, decays):
    scaling = query_rows.shape[1] ** (-0.5)
    running = jnp.cumsum(decays)
    block_total = running[-1]
    decay_mat = decay_matrix(running)
    weights = (jnp.dot(query_rows, key_rows.T, preferred_element_type=jnp.float32) * scaling * decay_mat).astype(jnp.bfloat16)
    head_decay = jnp.exp(running)
    query_decayed = (query_rows.astype(jnp.float32) * head_decay[:, None]).astype(jnp.bfloat16)
    tail_decay = jnp.exp(block_total - running)
    key_decayed = (key_rows.astype(jnp.float32) * tail_decay[:, None]).astype(jnp.bfloat16)
    local_state = jnp.dot(key_decayed.T, value_rows, preferred_element_type=jnp.float32)
    return (decay_mat, weights, head_decay, query_decayed, tail_decay, local_state, jnp.exp(block_total))

def norm_backward(terms, value_rows, state_in, upstream_rows, gain_row):
    decay_mat, weights, head_decay, query_decayed, tail_decay, local_state, block_decay = terms
    scaling = query_decayed.shape[1] ** (-0.5)
    state_low = state_in.astype(jnp.bfloat16)
    output = jnp.dot(weights, value_rows, preferred_element_type=jnp.float32) + scaling * jnp.dot(query_decayed, state_low, preferred_element_type=jnp.float32)
    centered = output - lax.optimization_barrier(jnp.mean(output, axis=-1, keepdims=True))
    inverse = lax.rsqrt(lax.optimization_barrier(jnp.mean(centered * centered, axis=-1, keepdims=True)) + norm_eps)
    normed = centered * inverse
    cotangent = upstream_rows.astype(jnp.float32)
    gain_part = lax.optimization_barrier(jnp.sum(cotangent * normed, axis=0))
    bias_part = lax.optimization_barrier(jnp.sum(cotangent, axis=0))
    scaled = cotangent * gain_row
    grad_output = (inverse * (scaled - lax.optimization_barrier(jnp.mean(scaled, axis=-1, keepdims=True)) - normed * lax.optimization_barrier(jnp.mean(scaled * normed, axis=-1, keepdims=True)))).astype(jnp.bfloat16)
    back_local = scaling * jnp.dot(query_decayed.T, grad_output, preferred_element_type=jnp.float32)
    return (grad_output, back_local, gain_part, bias_part)

def retention_backward(terms, query_rows, key_rows, value_rows, grad_output, state_in, state_after):
    decay_mat, weights, head_decay, query_decayed, tail_decay, local_state, block_decay = terms
    scaling = query_rows.shape[1] ** (-0.5)
    state_low = state_in.astype(jnp.bfloat16)
    after_low = state_after.astype(jnp.bfloat16)
    grad_weights = (jnp.dot(grad_output, value_rows.T, preferred_element_type=jnp.float32) * scaling * decay_mat).astype(jnp.bfloat16)
    query_grad = jnp.dot(grad_weights, key_rows, preferred_element_type=jnp.float32) + (scaling * head_decay)[:, None] * jnp.dot(grad_output, state_low.T, preferred_element_type=jnp.float32)
    key_grad = jnp.dot(grad_weights.T, query_rows, preferred_element_type=jnp.float32) + tail_decay[:, None] * jnp.dot(value_rows, after_low.T, preferred_element_type=jnp.float32)
    value_grad = jnp.dot(weights.T, grad_output, preferred_element_type=jnp.float32) + tail_decay[:, None] * jnp.dot(key_rows, after_low, preferred_element_type=jnp.float32)
    return (query_grad.astype(jnp.bfloat16), key_grad.astype(jnp.bfloat16), value_grad.astype(jnp.bfloat16))

def reference(queries, key_rows, value_rows, log_decay, upstream, norm_gain):
    head_count = norm_gain.shape[0]
    blocks = N_SEQ
    block_rows = queries.shape[0] // blocks
    key_width = queries.shape[1] // head_count
    value_width = value_rows.shape[1] // head_count

    def split_heads(array):
        head_width = array.shape[1] // head_count
        return array.reshape(blocks, block_rows, head_count, head_width).transpose(0, 2, 1, 3)

    def join_heads(array):
        head_width = array.shape[3]
        return array.transpose(0, 2, 1, 3).reshape(blocks * block_rows, head_count * head_width)
    query_blocks = split_heads(queries)
    key_blocks = split_heads(key_rows)
    value_blocks = split_heads(value_rows)
    upstream_blocks = split_heads(upstream)
    decay_blocks = log_decay.reshape(head_count, blocks, block_rows).transpose(1, 0, 2)
    state_shape = (head_count, key_width, value_width)

    def forward_step(carried, inputs):
        state_in, gain_total, bias_total = carried
        query_now, keys_now, values_now, decays_now, upstream_now = inputs

        def per_head(query_head, key_head, value_head, decay_head, cotangent, state_head, gain_head):
            terms = block_terms(query_head, key_head, value_head, decay_head)
            grad_output, back_local, gain_part, bias_part = norm_backward(terms, value_head, state_head, cotangent, gain_head)
            next_state = terms[6] * state_head + terms[5]
            return (next_state, grad_output, back_local, terms[6], gain_part, bias_part)
        results = jax.vmap(per_head)(query_now, keys_now, values_now, decays_now, upstream_now, state_in, norm_gain)
        next_state, grad_output, back_local, block_decay, gain_part, bias_part = results
        return ((next_state, gain_total + gain_part, bias_total + bias_part), (state_in, grad_output, back_local, block_decay))
    initial = (jnp.zeros(state_shape, jnp.float32), jnp.zeros(norm_gain.shape, jnp.float32), jnp.zeros(norm_gain.shape, jnp.float32))
    totals, stored = lax.scan(forward_step, initial, (query_blocks, key_blocks, value_blocks, decay_blocks, upstream_blocks))
    final_state, gain_total, bias_total = totals
    states_in, grad_outputs, back_locals, block_decays = stored

    def backward_step(state_after, inputs):
        query_now, keys_now, values_now, decays_now, grad_now, state_now, back_now, decay_now = inputs

        def per_head(query_head, key_head, value_head, decay_head, grad_head, state_head, after_head):
            terms = block_terms(query_head, key_head, value_head, decay_head)
            return retention_backward(terms, query_head, key_head, value_head, grad_head, state_head, after_head)
        gradients = jax.vmap(per_head)(query_now, keys_now, values_now, decays_now, grad_now, state_now, state_after)
        carried = back_now + decay_now[:, None, None] * state_after
        return (carried, gradients)
    leftover, gradients = lax.scan(backward_step, jnp.zeros(state_shape, jnp.float32), (query_blocks, key_blocks, value_blocks, decay_blocks, grad_outputs, states_in, back_locals, block_decays), reverse=True)
    norm_factor = queries.shape[0] ** (-0.5)
    return (join_heads(gradients[0]), join_heads(gradients[1]), join_heads(gradients[2]), gain_total * norm_factor, bias_total * norm_factor)
```

```python
import functools

import jax
import jax.numpy as jnp
from jax import lax
from jax.experimental import pallas as pl
from jax.experimental.pallas import tpu as pltpu
from jax.sharding import PartitionSpec as P

norm_eps = 1e-05
f32, bf16 = jnp.float32, jnp.bfloat16
PIECES = 2


def dot_nn(a, b):
    return lax.dot_general(a, b, (((1,), (0,)), ((), ())), preferred_element_type=f32)


def dot_nt(a, b):
    return lax.dot_general(a, b, (((1,), (1,)), ((), ())), preferred_element_type=f32)


def dot_tn(a, b):
    return lax.dot_general(a, b, (((0,), (0,)), ((), ())), preferred_element_type=f32)


def kernel(
    seq_total, head_total, members, pieces,
    q_hbm, k_hbm, v_hbm, decay_hbm, up_hbm, gain_hbm,
    qg_hbm, kg_hbm, vg_hbm, gg_hbm, bg_hbm,
    q_ref, k_ref, v_ref, decay_ref, gain_ref, up_ref, total_ref,
    lsend, lrecv, carry, csend, psend, state, stat_in, stat_z, stat_sum,
    qg_ref, kg_ref, vg_ref, gg_ref, bg_ref,
    load_sem, total_sem, up_sem, scatter_sem, chain_sem, spread_sem, stat_sem, statz_sem, out_sem,
):
    me = lax.axis_index("seq")
    head = lax.axis_index("head")
    groups = seq_total // members
    z = me // members
    r = me % members
    rows, dk = q_ref.shape
    dv = v_ref.shape[1]
    scaling = dk ** (-0.5)

    def member(d):
        return lax.rem(r + d, members)

    def remote(src, dst, sems, at, device):
        return pltpu.make_async_remote_copy(
            src_ref=src, dst_ref=dst, send_sem=sems.at[(0, *at)], recv_sem=sems.at[(1, *at)],
            device_id=device, device_id_type=pl.DeviceIdType.MESH,
        )

    def in_group(d):
        return {"seq": z * members + member(d)}

    def other_group(d):
        return {"seq": lax.rem(z + d, groups) * members + r}

    def other_head(d):
        return {"head": lax.rem(head + d, head_total)}

    up_own = up_hbm.at[:, pl.ds(pl.multiple_of(head * dv, dv), dv)]
    loads = [
        pltpu.make_async_copy(src, dst, load_sem.at[i])
        for i, (src, dst) in enumerate((
            (decay_hbm, decay_ref), (k_hbm, k_ref), (v_hbm, v_ref), (q_hbm, q_ref),
            (gain_hbm, gain_ref), (up_own, up_ref.at[head]),
        ))
    ]
    for load in loads:
        load.start()

    barrier = pltpu.get_barrier_semaphore()
    partners = (
        [in_group(d) for d in range(1, members)]
        + [other_group(d) for d in range(1, groups)]
        + [other_head(d) for d in range(1, head_total)]
    )
    for partner in partners:
        pl.semaphore_signal(barrier, inc=1, device_id=partner, device_id_type=pl.DeviceIdType.MESH)

    loads[0].wait()
    decays = decay_ref[...]
    at_row = lax.broadcasted_iota(jnp.int32, (rows, rows), 0)
    at_col = lax.broadcasted_iota(jnp.int32, (rows, rows), 1)
    lower = at_row >= at_col
    running = jnp.sum(jnp.where(lower, decays, 0.0), axis=1, keepdims=True)
    running_row = jnp.sum(jnp.where(at_row == at_col, running, 0.0), axis=0, keepdims=True)
    block_total = running[rows - 1 : rows, :]
    tail_decay = jnp.exp(block_total - running)
    head_decay = jnp.exp(running)
    total_ref[r] = jnp.broadcast_to(block_total, total_ref.shape[1:])
    loads[1].wait()
    loads[2].wait()
    keys, values = k_ref[...], v_ref[...]
    key_decayed = (keys.astype(f32) * tail_decay).astype(bf16)
    local_state = dot_tn(key_decayed, values)

    def scatter_copy(way, d, s):
        return remote(
            lsend.at[way, member(d), s], lrecv.at[way, r, s], scatter_sem, (way, d, s), in_group(d)
        )

    def scatter_arrival(way, d, s):
        return remote(
            lsend.at[way, member(d), s], lrecv.at[way, member(members - d), s], scatter_sem,
            (way, d, s), in_group(d),
        )

    def chain_copy(way, s):
        step = 1 if way == 0 else groups - 1
        return remote(csend.at[way, s], carry.at[way, s], chain_sem, (way, s), other_group(step))

    def spread_copy(way, d, s):
        return remote(
            psend.at[way, member(d), s], state.at[way, r, s], spread_sem, (way, d, s), in_group(d)
        )

    def spread_arrival(way, d, s):
        return remote(
            psend.at[way, member(d), s], state.at[way, member(members - d), s], spread_sem,
            (way, d, s), in_group(d),
        )

    def total_copy(d):
        return remote(total_ref.at[r], total_ref.at[r], total_sem, (d,), in_group(d))

    def total_arrival(d):
        slot = total_ref.at[member(members - d)]
        return remote(slot, slot, total_sem, (d,), in_group(d))

    def up_copy(d):
        whom = lax.rem(head + d, head_total)
        return remote(
            up_hbm.at[:, pl.ds(pl.multiple_of(whom * dv, dv), dv)], up_ref.at[head], up_sem, (d,),
            other_head(d),
        )

    def up_arrival(d):
        whom = lax.rem(head + head_total - d, head_total)
        return remote(up_hbm.at[:, pl.ds(0, dv)], up_ref.at[whom], up_sem, (d,), other_head(d))

    def stat_copy(d):
        return remote(stat_in.at[r], stat_in.at[r], stat_sem, (d,), in_group(d))

    def stat_arrival(d):
        slot = stat_in.at[member(members - d)]
        return remote(slot, slot, stat_sem, (d,), in_group(d))

    def statz_copy(d):
        return remote(stat_z.at[z], stat_z.at[z], statz_sem, (d,), other_group(d))

    def statz_arrival(d):
        slot = stat_z.at[lax.rem(z + groups - d, groups)]
        return remote(slot, slot, statz_sem, (d,), other_group(d))

    def scatter(way, local):
        lsend[way] = local.astype(bf16).reshape(lsend.shape[1:])
        for s in range(pieces):
            for d in range(1, members):
                scatter_copy(way, d, s).start()
        lrecv[way, r] = lsend[way, r]

    def chain(way, group_decays):
        order = range(members) if way == 0 else range(members - 1, -1, -1)
        first, last = (0, groups - 1) if way == 0 else (groups - 1, 0)
        whole = functools.reduce(lambda a, b: a * b, group_decays)

        @pl.when(z == first)
        def _():
            carry[way] = jnp.zeros(carry.shape[1:], bf16)

        for s in range(pieces):
            for d in range(1, members):
                scatter_arrival(way, d, s).wait_recv()
            total = None
            for m in order:
                part = lrecv[way, m, s].astype(f32)
                total = part if total is None else group_decays[m] * total + part

            @pl.when(z != first)
            def _():
                chain_copy(way, s).wait_recv()

            csend[way, s] = (whole * carry[way, s].astype(f32) + total).astype(bf16)

            @pl.when(z != last)
            def _():
                chain_copy(way, s).start()

            now = carry[way, s].astype(f32)
            for at, m in enumerate(order):
                psend[way, m, s] = now.astype(bf16)
                if at < members - 1:
                    now = group_decays[m] * now + lrecv[way, m, s].astype(f32)
            for d in range(1, members):
                spread_copy(way, d, s).start()
            state[way, r, s] = psend[way, r, s]

    def gathered(way):
        for s in range(pieces):
            for d in range(1, members):
                spread_arrival(way, d, s).wait_recv()
        return state[way].reshape(dk, dv)

    pl.semaphore_wait(barrier, len(partners))
    for d in range(1, members):
        total_copy(d).start()
    scatter(0, local_state)
    for d in range(1, head_total):
        up_copy(d).start()

    loads[3].wait()
    queries = q_ref[...]
    decay_mat = jnp.where(lower, jnp.exp(jnp.where(lower, running - running_row, 0.0)), 0.0)
    decay_mat = decay_mat * scaling
    weights = (dot_nt(queries, keys) * decay_mat).astype(bf16)
    query_decayed = (queries.astype(f32) * head_decay).astype(bf16)
    inner = dot_nn(weights, values)

    for d in range(1, members):
        total_arrival(d).wait_recv()
    group_decays = [jnp.exp(total_ref[m, 0:1, 0:1]) for m in range(members)]
    chain(0, group_decays)

    loads[4].wait()
    loads[5].wait()
    for d in range(1, head_total):
        up_arrival(d).wait_recv()
    cotangent = up_ref[...].reshape(rows, dv).astype(f32)
    scaled = cotangent * gain_ref[...]
    scaled_mean = jnp.mean(scaled, axis=-1, keepdims=True)

    state_in = gathered(0)
    output = inner + scaling * dot_nn(query_decayed, state_in)
    centered = output - jnp.mean(output, axis=-1, keepdims=True)
    inverse = lax.rsqrt(jnp.mean(centered * centered, axis=-1, keepdims=True) + norm_eps)
    normed = centered * inverse
    grad_output = (
        inverse * (scaled - scaled_mean - normed * jnp.mean(scaled * normed, axis=-1, keepdims=True))
    ).astype(bf16)
    scatter(1, scaling * dot_tn(query_decayed, grad_output))

    stat_in[r, 0:1, :] = jnp.sum(cotangent * normed, axis=0, keepdims=True)
    stat_in[r, 1:2, :] = jnp.sum(cotangent, axis=0, keepdims=True)
    for d in range(1, members):
        stat_copy(d).start()
    grad_weights = (dot_nt(grad_output, values) * decay_mat).astype(bf16)
    qg_ref[...] = (
        dot_nn(grad_weights, keys) + (scaling * head_decay) * dot_nt(grad_output, state_in)
    ).astype(bf16)
    outs = [
        pltpu.make_async_copy(src, dst, out_sem.at[i])
        for i, (src, dst) in enumerate((
            (qg_ref, qg_hbm), (kg_ref, kg_hbm), (vg_ref, vg_hbm), (gg_ref, gg_hbm), (bg_ref, bg_hbm),
        ))
    ]
    outs[0].start()

    chain(1, group_decays)

    key_inner = dot_tn(grad_weights, queries)
    value_inner = dot_tn(weights, grad_output)
    for d in range(1, members):
        stat_arrival(d).wait_recv()
    both = stat_in[0]
    for m in range(1, members):
        both = both + stat_in[m]
    stat_z[z] = both
    for d in range(1, groups):
        statz_copy(d).start()

    state_after = gathered(1)
    kg_ref[...] = (key_inner + tail_decay * dot_nt(values, state_after)).astype(bf16)
    outs[1].start()
    vg_ref[...] = (value_inner + tail_decay * dot_nn(keys, state_after)).astype(bf16)
    outs[2].start()

    for d in range(1, groups):
        statz_arrival(d).wait_recv()
    both = stat_z[0]
    for m in range(1, groups):
        both = both + stat_z[m]
    both = both * ((rows * seq_total) ** (-0.5))
    gg_ref[...] = both[0:1, :]
    bg_ref[...] = both[1:2, :]
    outs[3].start()
    outs[4].start()

    for d in range(1, members):
        total_copy(d).wait_send()
        stat_copy(d).wait_send()
        for way in range(2):
            for s in range(pieces):
                scatter_copy(way, d, s).wait_send()
                spread_copy(way, d, s).wait_send()
    for d in range(1, head_total):
        up_copy(d).wait_send()
    for d in range(1, groups):
        statz_copy(d).wait_send()
    for way, last in ((0, groups - 1), (1, 0)):

        @pl.when(z != last)
        def _():
            for s in range(pieces):
                chain_copy(way, s).wait_send()

    for out in outs:
        out.wait()


def shards(queries, key_rows, value_rows, log_decay, upstream, norm_gain):
    seq_total, head_total = lax.axis_size("seq"), lax.axis_size("head")
    members = 4 if seq_total % 4 == 0 else 1
    groups = seq_total // members
    rows, dk = queries.shape
    dv = value_rows.shape[1]
    pieces = PIECES
    piece = (pieces, dk // members // pieces, dv)
    any_space = pl.BlockSpec(memory_space=pl.ANY)
    dma = pltpu.SemaphoreType.DMA
    return pl.pallas_call(
        functools.partial(kernel, seq_total, head_total, members, pieces),
        out_shape=(
            jax.ShapeDtypeStruct((rows, dk), bf16),
            jax.ShapeDtypeStruct((rows, dk), bf16),
            jax.ShapeDtypeStruct((rows, dv), bf16),
            jax.ShapeDtypeStruct((1, dv), f32),
            jax.ShapeDtypeStruct((1, dv), f32),
        ),
        in_specs=[any_space] * 6,
        out_specs=(any_space,) * 5,
        scratch_shapes=[
            pltpu.VMEM((rows, dk), bf16),
            pltpu.VMEM((rows, dk), bf16),
            pltpu.VMEM((rows, dv), bf16),
            pltpu.VMEM((1, rows), f32),
            pltpu.VMEM((1, dv), f32),
            pltpu.VMEM((head_total, rows // head_total, dv), bf16),
            pltpu.VMEM((members, 8, 128), f32),
            pltpu.VMEM((2, members, *piece), bf16),
            pltpu.VMEM((2, members, *piece), bf16),
            pltpu.VMEM((2, *piece), bf16),
            pltpu.VMEM((2, *piece), bf16),
            pltpu.VMEM((2, members, *piece), bf16),
            pltpu.VMEM((2, members, *piece), bf16),
            pltpu.VMEM((members, 2, dv), f32),
            pltpu.VMEM((groups, 2, dv), f32),
            pltpu.VMEM((8, dv), f32),
            pltpu.VMEM((rows, dk), bf16),
            pltpu.VMEM((rows, dk), bf16),
            pltpu.VMEM((rows, dv), bf16),
            pltpu.VMEM((1, dv), f32),
            pltpu.VMEM((1, dv), f32),
            dma((6,)),
            dma((2, members)),
            dma((2, max(head_total, 2))),
            dma((2, 2, members, pieces)),
            dma((2, 2, pieces)),
            dma((2, 2, members, pieces)),
            dma((2, members)),
            dma((2, max(groups, 2))),
            dma((5,)),
        ],
        compiler_params=pltpu.CompilerParams(
            collective_id=0, has_side_effects=True, vmem_limit_bytes=40 * 2**20
        ),
    )(queries, key_rows, value_rows, log_decay, upstream, norm_gain)


def solution(mesh):
    in_specs = (
        P("seq", "head"),
        P("seq", "head"),
        P("seq", "head"),
        P("head", "seq"),
        P(("seq", "head"), None),
        P("head", None),
    )
    out_specs = (
        P("seq", "head"),
        P("seq", "head"),
        P("seq", "head"),
        P("head", None),
        P("head", None),
    )
    return jax.shard_map(shards, mesh=mesh, in_specs=in_specs, out_specs=out_specs, check_vma=False)
```

```python
import functools

import jax
import jax.numpy as jnp
from jax import lax
from jax.experimental import pallas as pl
from jax.experimental.pallas import tpu as pltpu
from jax.sharding import PartitionSpec as P

norm_eps = 1e-05
f32, bf16 = jnp.float32, jnp.bfloat16
PIECES = 4


def dot_nn(a, b):
    return lax.dot_general(a, b, (((1,), (0,)), ((), ())), preferred_element_type=f32)


def dot_nt(a, b):
    return lax.dot_general(a, b, (((1,), (1,)), ((), ())), preferred_element_type=f32)


def dot_tn(a, b):
    return lax.dot_general(a, b, (((0,), (0,)), ((), ())), preferred_element_type=f32)


def kernel(
    seq_total, head_total, members, pieces,
    q_hbm, k_hbm, v_hbm, decay_hbm, up_hbm, gain_hbm,
    qg_ref, kg_ref, vg_ref, gg_ref, bg_ref,
    q_ref, k_ref, v_ref, decay_ref, gain_ref, up_ref, total_ref,
    turned, lsend, lrecv, carry, csend, psend, state, stat_in, stat_z, stat_sum,
    load_sem, total_sem, up_sem, scatter_sem, chain_sem, spread_sem, stat_sem, statz_sem,
):
    me = lax.axis_index("seq")
    head = lax.axis_index("head")
    groups = seq_total // members
    z = me // members
    r = me % members
    rows, dk = q_ref.shape
    dv = v_ref.shape[1]
    scaling = dk ** (-0.5)

    def member(d):
        return lax.rem(r + d, members)

    def remote(src, dst, sems, at, device):
        return pltpu.make_async_remote_copy(
            src_ref=src, dst_ref=dst, send_sem=sems.at[(0, *at)], recv_sem=sems.at[(1, *at)],
            device_id=device, device_id_type=pl.DeviceIdType.MESH,
        )

    def in_group(d):
        return {"seq": z * members + member(d)}

    def other_group(d):
        return {"seq": lax.rem(z + d, groups) * members + r}

    def other_head(d):
        return {"head": lax.rem(head + d, head_total)}

    up_own = up_hbm.at[:, pl.ds(pl.multiple_of(head * dv, dv), dv)]
    loads = [
        pltpu.make_async_copy(src, dst, load_sem.at[i])
        for i, (src, dst) in enumerate((
            (decay_hbm, decay_ref), (k_hbm, k_ref), (v_hbm, v_ref), (q_hbm, q_ref),
            (gain_hbm, gain_ref), (up_own, up_ref.at[head]),
        ))
    ]
    for load in loads:
        load.start()

    barrier = pltpu.get_barrier_semaphore()
    partners = (
        [in_group(d) for d in range(1, members)]
        + [other_group(d) for d in range(1, groups)]
        + [other_head(d) for d in range(1, head_total)]
    )
    for partner in partners:
        pl.semaphore_signal(barrier, inc=1, device_id=partner, device_id_type=pl.DeviceIdType.MESH)

    loads[0].wait()
    decays = decay_ref[...]
    at_row = lax.broadcasted_iota(jnp.int32, (rows, rows), 0)
    at_col = lax.broadcasted_iota(jnp.int32, (rows, rows), 1)
    lower = at_row >= at_col
    running = jnp.sum(jnp.where(lower, decays, 0.0), axis=1, keepdims=True)
    running_row = jnp.sum(jnp.where(at_row == at_col, running, 0.0), axis=0, keepdims=True)
    block_total = running[rows - 1 : rows, :]
    tail_decay = jnp.exp(block_total - running)
    head_decay = jnp.exp(running)
    total_ref[r] = jnp.broadcast_to(block_total, total_ref.shape[1:])
    loads[1].wait()
    loads[2].wait()
    keys, values = k_ref[...], v_ref[...]
    key_decayed = (keys.astype(f32) * tail_decay).astype(bf16)
    turned[0] = key_decayed.T.reshape(turned.shape[1:])

    def scatter_copy(way, d, s):
        return remote(
            lsend.at[way, member(d), s], lrecv.at[way, r, s], scatter_sem, (way, d, s), in_group(d)
        )

    def scatter_arrival(way, d, s):
        return remote(
            lsend.at[way, member(d), s], lrecv.at[way, member(members - d), s], scatter_sem,
            (way, d, s), in_group(d),
        )

    def chain_copy(way, s):
        step = 1 if way == 0 else groups - 1
        return remote(csend.at[way, s], carry.at[way, s], chain_sem, (way, s), other_group(step))

    def spread_copy(way, d, s):
        return remote(
            psend.at[way, member(d), s], state.at[way, r, s], spread_sem, (way, d, s), in_group(d)
        )

    def spread_arrival(way, d, s):
        return remote(
            psend.at[way, member(d), s], state.at[way, member(members - d), s], spread_sem,
            (way, d, s), in_group(d),
        )

    def total_copy(d):
        return remote(total_ref.at[r], total_ref.at[r], total_sem, (d,), in_group(d))

    def total_arrival(d):
        slot = total_ref.at[member(members - d)]
        return remote(slot, slot, total_sem, (d,), in_group(d))

    def up_copy(d):
        whom = lax.rem(head + d, head_total)
        return remote(
            up_hbm.at[:, pl.ds(pl.multiple_of(whom * dv, dv), dv)], up_ref.at[head], up_sem, (d,),
            other_head(d),
        )

    def up_arrival(d):
        whom = lax.rem(head + head_total - d, head_total)
        return remote(up_hbm.at[:, pl.ds(0, dv)], up_ref.at[whom], up_sem, (d,), other_head(d))

    def stat_copy(d):
        return remote(stat_in.at[r], stat_in.at[r], stat_sem, (d,), in_group(d))

    def stat_arrival(d):
        slot = stat_in.at[member(members - d)]
        return remote(slot, slot, stat_sem, (d,), in_group(d))

    def statz_copy(d):
        return remote(stat_z.at[z], stat_z.at[z], statz_sem, (d,), other_group(d))

    def statz_arrival(d):
        slot = stat_z.at[lax.rem(z + groups - d, groups)]
        return remote(slot, slot, statz_sem, (d,), other_group(d))

    def scatter(way, right):
        for d in [members // 2, *(d for d in range(1, members) if d != members // 2), 0]:
            part = dot_nn(turned[way, member(d)], right).astype(bf16).reshape(lsend.shape[2:])
            if d:
                lsend[way, member(d)] = part
                for s in range(pieces):
                    scatter_copy(way, d, s).start()
            else:
                lrecv[way, r] = part

    def chain(way, group_decays):
        order = range(members) if way == 0 else range(members - 1, -1, -1)
        first, last = (0, groups - 1) if way == 0 else (groups - 1, 0)
        whole = functools.reduce(lambda a, b: a * b, group_decays)

        @pl.when(z == first)
        def _():
            carry[way] = jnp.zeros(carry.shape[1:], bf16)

        for s in range(pieces):
            for d in range(1, members):
                scatter_arrival(way, d, s).wait_recv()
            total = None
            for m in order:
                part = lrecv[way, m, s].astype(f32)
                total = part if total is None else group_decays[m] * total + part

            @pl.when(z != first)
            def _():
                chain_copy(way, s).wait_recv()

            csend[way, s] = (whole * carry[way, s].astype(f32) + total).astype(bf16)

            @pl.when(z != last)
            def _():
                chain_copy(way, s).start()

            now = carry[way, s].astype(f32)
            for at, m in enumerate(order):
                psend[way, m, s] = now.astype(bf16)
                if at < members - 1:
                    now = group_decays[m] * now + lrecv[way, m, s].astype(f32)
            for d in range(1, members):
                spread_copy(way, d, s).start()
            state[way, r, s] = psend[way, r, s]

    def gathered(way):
        for s in range(pieces):
            for d in range(1, members):
                spread_arrival(way, d, s).wait_recv()
        return state[way].reshape(dk, dv)

    pl.semaphore_wait(barrier, len(partners))
    for d in range(1, members):
        total_copy(d).start()
    scatter(0, values)
    for d in range(1, head_total):
        up_copy(d).start()

    loads[3].wait()
    queries = q_ref[...]
    decay_mat = jnp.where(lower, jnp.exp(jnp.where(lower, running - running_row, 0.0)), 0.0)
    decay_mat = decay_mat * scaling
    weights = (dot_nt(queries, keys) * decay_mat).astype(bf16)
    query_decayed = (queries.astype(f32) * head_decay).astype(bf16)
    inner = dot_nn(weights, values)
    turned[1] = (scaling * query_decayed.astype(f32)).astype(bf16).T.reshape(turned.shape[1:])

    for d in range(1, members):
        total_arrival(d).wait_recv()
    group_decays = [jnp.exp(total_ref[m, 0:1, 0:1]) for m in range(members)]
    chain(0, group_decays)

    loads[4].wait()
    loads[5].wait()
    for d in range(1, head_total):
        up_arrival(d).wait_recv()
    cotangent = up_ref[...].reshape(rows, dv).astype(f32)
    scaled = cotangent * gain_ref[...]
    scaled_mean = jnp.mean(scaled, axis=-1, keepdims=True)

    state_in = gathered(0)
    output = inner + scaling * dot_nn(query_decayed, state_in)
    centered = output - jnp.mean(output, axis=-1, keepdims=True)
    along = jnp.mean(scaled * centered, axis=-1, keepdims=True)
    inverse = lax.rsqrt(jnp.mean(centered * centered, axis=-1, keepdims=True) + norm_eps)
    normed = centered * inverse
    grad_output = (inverse * (scaled - scaled_mean - normed * (along * inverse))).astype(bf16)
    scatter(1, grad_output)

    stat_in[r, 0:1, :] = jnp.sum(cotangent * normed, axis=0, keepdims=True)
    stat_in[r, 1:2, :] = jnp.sum(cotangent, axis=0, keepdims=True)
    for d in range(1, members):
        stat_copy(d).start()
    grad_weights = (dot_nt(grad_output, values) * decay_mat).astype(bf16)
    qg_ref[...] = (
        dot_nn(grad_weights, keys) + (scaling * head_decay) * dot_nt(grad_output, state_in)
    ).astype(bf16)
    chain(1, group_decays)

    key_inner = dot_tn(grad_weights, queries)
    value_inner = dot_tn(weights, grad_output)
    for d in range(1, members):
        stat_arrival(d).wait_recv()
    both = stat_in[0]
    for m in range(1, members):
        both = both + stat_in[m]
    stat_z[z] = both
    for d in range(1, groups):
        statz_copy(d).start()

    state_after = gathered(1)
    kg_ref[...] = (key_inner + tail_decay * dot_nt(values, state_after)).astype(bf16)
    vg_ref[...] = (value_inner + tail_decay * dot_nn(keys, state_after)).astype(bf16)

    for d in range(1, groups):
        statz_arrival(d).wait_recv()
    both = stat_z[0]
    for m in range(1, groups):
        both = both + stat_z[m]
    both = both * ((rows * seq_total) ** (-0.5))
    gg_ref[...] = both[0:1, :]
    bg_ref[...] = both[1:2, :]

    for d in range(1, members):
        total_copy(d).wait_send()
        stat_copy(d).wait_send()
        for way in range(2):
            for s in range(pieces):
                scatter_copy(way, d, s).wait_send()
                spread_copy(way, d, s).wait_send()
    for d in range(1, head_total):
        up_copy(d).wait_send()
    for d in range(1, groups):
        statz_copy(d).wait_send()
    for way, last in ((0, groups - 1), (1, 0)):

        @pl.when(z != last)
        def _():
            for s in range(pieces):
                chain_copy(way, s).wait_send()


def write_out(*refs):
    *pairs, sems = refs
    half = len(pairs) // 2
    copies = [
        pltpu.make_async_copy(src, dst, sems.at[i])
        for i, (src, dst) in enumerate(zip(pairs[:half], pairs[half:]))
    ]
    for copy in copies:
        copy.start()
    for copy in copies:
        copy.wait()


def shards(queries, key_rows, value_rows, log_decay, upstream, norm_gain):
    seq_total, head_total = lax.axis_size("seq"), lax.axis_size("head")
    members = 4 if seq_total % 4 == 0 else 1
    groups = seq_total // members
    rows, dk = queries.shape
    dv = value_rows.shape[1]
    pieces = PIECES
    piece = (pieces, dk // members // pieces, dv)
    in_hbm = pl.BlockSpec(memory_space=pltpu.HBM)
    in_vmem = pl.BlockSpec(memory_space=pltpu.VMEM)
    shapes = (
        jax.ShapeDtypeStruct((rows, dk), bf16),
        jax.ShapeDtypeStruct((rows, dk), bf16),
        jax.ShapeDtypeStruct((rows, dv), bf16),
        jax.ShapeDtypeStruct((1, dv), f32),
        jax.ShapeDtypeStruct((1, dv), f32),
    )
    dma = pltpu.SemaphoreType.DMA
    results = pl.pallas_call(
        functools.partial(kernel, seq_total, head_total, members, pieces),
        out_shape=shapes,
        in_specs=[in_hbm] * 6,
        out_specs=(in_vmem,) * 5,
        scratch_shapes=[
            pltpu.VMEM((rows, dk), bf16),
            pltpu.VMEM((rows, dk), bf16),
            pltpu.VMEM((rows, dv), bf16),
            pltpu.VMEM((1, rows), f32),
            pltpu.VMEM((1, dv), f32),
            pltpu.VMEM((head_total, rows // head_total, dv), bf16),
            pltpu.VMEM((members, 8, 128), f32),
            pltpu.VMEM((2, members, dk // members, rows), bf16),
            pltpu.VMEM((2, members, *piece), bf16),
            pltpu.VMEM((2, members, *piece), bf16),
            pltpu.VMEM((2, *piece), bf16),
            pltpu.VMEM((2, *piece), bf16),
            pltpu.VMEM((2, members, *piece), bf16),
            pltpu.VMEM((2, members, *piece), bf16),
            pltpu.VMEM((members, 2, dv), f32),
            pltpu.VMEM((groups, 2, dv), f32),
            pltpu.VMEM((8, dv), f32),
            dma((6,)),
            dma((2, members)),
            dma((2, max(head_total, 2))),
            dma((2, 2, members, pieces)),
            dma((2, 2, pieces)),
            dma((2, 2, members, pieces)),
            dma((2, members)),
            dma((2, max(groups, 2))),
        ],
        compiler_params=pltpu.CompilerParams(
            collective_id=0, has_side_effects=True, vmem_limit_bytes=62 * 2**20
        ),
    )(queries, key_rows, value_rows, log_decay, upstream, norm_gain)
    return pl.pallas_call(
        write_out,
        out_shape=shapes,
        in_specs=[in_vmem] * 5,
        out_specs=(in_hbm,) * 5,
        scratch_shapes=[dma((5,))],
        compiler_params=pltpu.CompilerParams(vmem_limit_bytes=62 * 2**20),
    )(*results)


def solution(mesh):
    in_specs = (
        P("seq", "head"),
        P("seq", "head"),
        P("seq", "head"),
        P("head", "seq"),
        P(("seq", "head"), None),
        P("head", None),
    )
    out_specs = (
        P("seq", "head"),
        P("seq", "head"),
        P("seq", "head"),
        P("head", None),
        P("head", None),
    )
    return jax.shard_map(shards, mesh=mesh, in_specs=in_specs, out_specs=out_specs, check_vma=False)
```

```python
import functools

import jax
import jax.numpy as jnp
from jax import lax
from jax.experimental import pallas as pl
from jax.experimental.pallas import tpu as pltpu
from jax.sharding import PartitionSpec as P

norm_eps = 1e-05
f32, bf16 = jnp.float32, jnp.bfloat16
PIECES = 4


def dot_nn(a, b):
    return lax.dot_general(a, b, (((1,), (0,)), ((), ())), preferred_element_type=f32)


def dot_nt(a, b):
    return lax.dot_general(a, b, (((1,), (1,)), ((), ())), preferred_element_type=f32)


def dot_tn(a, b):
    return lax.dot_general(a, b, (((0,), (0,)), ((), ())), preferred_element_type=f32)


def kernel(
    seq_total, head_total, members, pieces,
    q_hbm, k_hbm, v_hbm, decay_hbm, up_hbm, gain_hbm,
    qg_ref, kg_ref, vg_ref, gg_ref, bg_ref,
    q_ref, k_ref, v_ref, decay_ref, gain_ref, up_ref, total_ref, span_ref,
    turned, lsend, lrecv, carry, csend, psend, state, stat_in, stat_z, stat_sum,
    load_sem, total_sem, up_sem, scatter_sem, chain_sem, spread_sem, stat_sem, statz_sem, span_sem,
):
    me = lax.axis_index("seq")
    head = lax.axis_index("head")
    groups = seq_total // members
    z = me // members
    r = me % members
    rows, dk = q_ref.shape
    dv = v_ref.shape[1]
    scaling = dk ** (-0.5)

    def member(d):
        return lax.rem(r + d, members)

    def remote(src, dst, sems, at, device):
        return pltpu.make_async_remote_copy(
            src_ref=src, dst_ref=dst, send_sem=sems.at[(0, *at)], recv_sem=sems.at[(1, *at)],
            device_id=device, device_id_type=pl.DeviceIdType.MESH,
        )

    def in_group(d):
        return {"seq": z * members + member(d)}

    def other_group(d):
        return {"seq": lax.rem(z + d, groups) * members + r}

    def other_head(d):
        return {"head": lax.rem(head + d, head_total)}

    up_own = up_hbm.at[:, pl.ds(pl.multiple_of(head * dv, dv), dv)]
    loads = [
        pltpu.make_async_copy(src, dst, load_sem.at[i])
        for i, (src, dst) in enumerate((
            (decay_hbm, decay_ref), (k_hbm, k_ref), (v_hbm, v_ref), (q_hbm, q_ref),
            (gain_hbm, gain_ref), (up_own, up_ref.at[head]),
        ))
    ]
    for load in loads:
        load.start()

    barrier = pltpu.get_barrier_semaphore()
    partners = (
        [in_group(d) for d in range(1, members)]
        + [other_group(d) for d in range(1, groups)]
        + [other_head(d) for d in range(1, head_total)]
    )
    for partner in partners:
        pl.semaphore_signal(barrier, inc=1, device_id=partner, device_id_type=pl.DeviceIdType.MESH)

    loads[0].wait()
    decays = decay_ref[...]
    at_row = lax.broadcasted_iota(jnp.int32, (rows, rows), 0)
    at_col = lax.broadcasted_iota(jnp.int32, (rows, rows), 1)
    lower = at_row >= at_col
    running = jnp.sum(jnp.where(lower, decays, 0.0), axis=1, keepdims=True)
    running_row = jnp.sum(jnp.where(at_row == at_col, running, 0.0), axis=0, keepdims=True)
    block_total = running[rows - 1 : rows, :]
    tail_decay = jnp.exp(block_total - running)
    head_decay = jnp.exp(running)
    total_ref[r] = jnp.broadcast_to(block_total, total_ref.shape[1:])
    loads[1].wait()
    loads[2].wait()
    keys, values = k_ref[...], v_ref[...]
    key_decayed = (keys.astype(f32) * tail_decay).astype(bf16)
    turned[0] = key_decayed.T.reshape(turned.shape[1:])

    def scatter_copy(way, d, s):
        return remote(
            lsend.at[way, member(d), s], lrecv.at[way, r, s], scatter_sem, (way, d, s), in_group(d)
        )

    def scatter_arrival(way, d, s):
        return remote(
            lsend.at[way, member(d), s], lrecv.at[way, member(members - d), s], scatter_sem,
            (way, d, s), in_group(d),
        )

    def sends_to(way, d):
        return z + d < groups if way == 0 else z - d >= 0

    def chain_copy(way, d, s):
        return remote(
            csend.at[way, s], carry.at[way, z, s], chain_sem, (way, d, s),
            other_group(d if way == 0 else groups - d),
        )

    def chain_arrival(way, d, s):
        source = lax.rem(z + (groups - d if way == 0 else d), groups)
        return remote(
            csend.at[way, s], carry.at[way, source, s], chain_sem, (way, d, s),
            other_group(d if way == 0 else groups - d),
        )

    def span_copy(d):
        return remote(span_ref.at[z], span_ref.at[z], span_sem, (d,), other_group(d))

    def span_arrival(d):
        slot = span_ref.at[lax.rem(z + groups - d, groups)]
        return remote(slot, slot, span_sem, (d,), other_group(d))

    def spread_copy(way, d, s):
        return remote(
            psend.at[way, member(d), s], state.at[way, r, s], spread_sem, (way, d, s), in_group(d)
        )

    def spread_arrival(way, d, s):
        return remote(
            psend.at[way, member(d), s], state.at[way, member(members - d), s], spread_sem,
            (way, d, s), in_group(d),
        )

    def total_copy(d):
        return remote(total_ref.at[r], total_ref.at[r], total_sem, (d,), in_group(d))

    def total_arrival(d):
        slot = total_ref.at[member(members - d)]
        return remote(slot, slot, total_sem, (d,), in_group(d))

    def up_copy(d):
        whom = lax.rem(head + d, head_total)
        return remote(
            up_hbm.at[:, pl.ds(pl.multiple_of(whom * dv, dv), dv)], up_ref.at[head], up_sem, (d,),
            other_head(d),
        )

    def up_arrival(d):
        whom = lax.rem(head + head_total - d, head_total)
        return remote(up_hbm.at[:, pl.ds(0, dv)], up_ref.at[whom], up_sem, (d,), other_head(d))

    def stat_copy(d):
        return remote(stat_in.at[r], stat_in.at[r], stat_sem, (d,), in_group(d))

    def stat_arrival(d):
        slot = stat_in.at[member(members - d)]
        return remote(slot, slot, stat_sem, (d,), in_group(d))

    def statz_copy(d):
        return remote(stat_z.at[z], stat_z.at[z], statz_sem, (d,), other_group(d))

    def statz_arrival(d):
        slot = stat_z.at[lax.rem(z + groups - d, groups)]
        return remote(slot, slot, statz_sem, (d,), other_group(d))

    def scatter(way, right):
        for d in [members // 2, *(d for d in range(1, members) if d != members // 2), 0]:
            part = dot_nn(turned[way, member(d)], right).astype(bf16).reshape(lsend.shape[2:])
            if d:
                lsend[way, member(d)] = part
                for s in range(pieces):
                    scatter_copy(way, d, s).start()
            else:
                lrecv[way, r] = part

    def chain(way, group_decays):
        order = range(members) if way == 0 else range(members - 1, -1, -1)
        for other in range(groups):

            @pl.when(other >= z if way == 0 else other <= z)
            def _():
                carry[way, other] = jnp.zeros(carry.shape[2:], bf16)

        for s in range(pieces):
            for d in range(1, members):
                scatter_arrival(way, d, s).wait_recv()
            total = None
            for m in order:
                part = lrecv[way, m, s].astype(f32)
                total = part if total is None else group_decays[m] * total + part
            csend[way, s] = total.astype(bf16)
            for d in range(1, groups):

                @pl.when(sends_to(way, d))
                def _():
                    chain_copy(way, d, s).start()

        if way == 0:
            for d in range(1, groups):
                span_arrival(d).wait_recv()
        spans = []
        for other in range(groups):
            ahead = other < z if way == 0 else other > z
            spans.append(jnp.exp(jnp.where(ahead, span_ref[other, 0:1, 0:1], 0.0)))
        for s in range(pieces):
            for d in range(1, groups):

                @pl.when(sends_to(1 - way, d))
                def _():
                    chain_arrival(way, d, s).wait_recv()

            now = jnp.zeros(carry.shape[3:], f32)
            for other in range(groups) if way == 0 else range(groups - 1, -1, -1):
                now = spans[other] * now + carry[way, other, s].astype(f32)
            for at, m in enumerate(order):
                psend[way, m, s] = now.astype(bf16)
                if at < members - 1:
                    now = group_decays[m] * now + lrecv[way, m, s].astype(f32)
            for d in [members // 2, *(d for d in range(1, members) if d != members // 2)]:
                spread_copy(way, d, s).start()
            state[way, r, s] = psend[way, r, s]

    def gathered(way):
        for s in range(pieces):
            for d in range(1, members):
                spread_arrival(way, d, s).wait_recv()
        return state[way].reshape(dk, dv)

    pl.semaphore_wait(barrier, len(partners))
    for d in range(1, members):
        total_copy(d).start()
    scatter(0, values)
    for d in range(1, head_total):
        up_copy(d).start()

    loads[3].wait()
    queries = q_ref[...]
    decay_mat = jnp.where(lower, jnp.exp(jnp.where(lower, running - running_row, 0.0)), 0.0)
    decay_mat = decay_mat * scaling
    weights = (dot_nt(queries, keys) * decay_mat).astype(bf16)
    query_decayed = (queries.astype(f32) * head_decay).astype(bf16)
    inner = dot_nn(weights, values)
    turned[1] = (scaling * query_decayed.astype(f32)).astype(bf16).T.reshape(turned.shape[1:])

    for d in range(1, members):
        total_arrival(d).wait_recv()
    group_decays = [jnp.exp(total_ref[m, 0:1, 0:1]) for m in range(members)]
    span = total_ref[0]
    for m in range(1, members):
        span = span + total_ref[m]
    span_ref[z] = span
    for d in range(1, groups):
        span_copy(d).start()
    chain(0, group_decays)

    loads[4].wait()
    loads[5].wait()
    for d in range(1, head_total):
        up_arrival(d).wait_recv()
    cotangent = up_ref[...].reshape(rows, dv).astype(f32)
    scaled = cotangent * gain_ref[...]
    scaled_mean = jnp.mean(scaled, axis=-1, keepdims=True)

    state_in = gathered(0)
    output = inner + scaling * dot_nn(query_decayed, state_in)
    centered = output - jnp.mean(output, axis=-1, keepdims=True)
    along = jnp.mean(scaled * centered, axis=-1, keepdims=True)
    inverse = lax.rsqrt(jnp.mean(centered * centered, axis=-1, keepdims=True) + norm_eps)
    normed = centered * inverse
    grad_output = (inverse * (scaled - scaled_mean - normed * (along * inverse))).astype(bf16)
    scatter(1, grad_output)

    stat_in[r, 0:1, :] = jnp.sum(cotangent * normed, axis=0, keepdims=True)
    stat_in[r, 1:2, :] = jnp.sum(cotangent, axis=0, keepdims=True)
    for d in range(1, members):
        stat_copy(d).start()
    grad_weights = (dot_nt(grad_output, values) * decay_mat).astype(bf16)
    qg_ref[...] = (
        dot_nn(grad_weights, keys) + (scaling * head_decay) * dot_nt(grad_output, state_in)
    ).astype(bf16)
    chain(1, group_decays)

    key_inner = dot_tn(grad_weights, queries)
    value_inner = dot_tn(weights, grad_output)
    for d in range(1, members):
        stat_arrival(d).wait_recv()
    both = stat_in[0]
    for m in range(1, members):
        both = both + stat_in[m]
    stat_z[z] = both
    for d in range(1, groups):
        statz_copy(d).start()

    state_after = gathered(1)
    kg_ref[...] = (key_inner + tail_decay * dot_nt(values, state_after)).astype(bf16)
    vg_ref[...] = (value_inner + tail_decay * dot_nn(keys, state_after)).astype(bf16)

    for d in range(1, groups):
        statz_arrival(d).wait_recv()
    both = stat_z[0]
    for m in range(1, groups):
        both = both + stat_z[m]
    both = both * ((rows * seq_total) ** (-0.5))
    gg_ref[...] = both[0:1, :]
    bg_ref[...] = both[1:2, :]

    for d in range(1, members):
        total_copy(d).wait_send()
        stat_copy(d).wait_send()
        for way in range(2):
            for s in range(pieces):
                scatter_copy(way, d, s).wait_send()
                spread_copy(way, d, s).wait_send()
    for d in range(1, head_total):
        up_copy(d).wait_send()
    for d in range(1, groups):
        statz_copy(d).wait_send()
        span_copy(d).wait_send()
    for way in range(2):
        for d in range(1, groups):

            @pl.when(sends_to(way, d))
            def _():
                for s in range(pieces):
                    chain_copy(way, d, s).wait_send()


def write_out(*refs):
    *pairs, sems = refs
    half = len(pairs) // 2
    copies = [
        pltpu.make_async_copy(src, dst, sems.at[i])
        for i, (src, dst) in enumerate(zip(pairs[:half], pairs[half:]))
    ]
    for copy in copies:
        copy.start()
    for copy in copies:
        copy.wait()


def shards(queries, key_rows, value_rows, log_decay, upstream, norm_gain):
    seq_total, head_total = lax.axis_size("seq"), lax.axis_size("head")
    members = 4 if seq_total % 4 == 0 else 1
    groups = seq_total // members
    rows, dk = queries.shape
    dv = value_rows.shape[1]
    pieces = PIECES
    piece = (pieces, dk // members // pieces, dv)
    in_hbm = pl.BlockSpec(memory_space=pltpu.HBM)
    in_vmem = pl.BlockSpec(memory_space=pltpu.VMEM)
    shapes = (
        jax.ShapeDtypeStruct((rows, dk), bf16),
        jax.ShapeDtypeStruct((rows, dk), bf16),
        jax.ShapeDtypeStruct((rows, dv), bf16),
        jax.ShapeDtypeStruct((1, dv), f32),
        jax.ShapeDtypeStruct((1, dv), f32),
    )
    dma = pltpu.SemaphoreType.DMA
    results = pl.pallas_call(
        functools.partial(kernel, seq_total, head_total, members, pieces),
        out_shape=shapes,
        in_specs=[in_hbm] * 6,
        out_specs=(in_vmem,) * 5,
        scratch_shapes=[
            pltpu.VMEM((rows, dk), bf16),
            pltpu.VMEM((rows, dk), bf16),
            pltpu.VMEM((rows, dv), bf16),
            pltpu.VMEM((1, rows), f32),
            pltpu.VMEM((1, dv), f32),
            pltpu.VMEM((head_total, rows // head_total, dv), bf16),
            pltpu.VMEM((members, 8, 128), f32),
            pltpu.VMEM((groups, 8, 128), f32),
            pltpu.VMEM((2, members, dk // members, rows), bf16),
            pltpu.VMEM((2, members, *piece), bf16),
            pltpu.VMEM((2, members, *piece), bf16),
            pltpu.VMEM((2, groups, *piece), bf16),
            pltpu.VMEM((2, *piece), bf16),
            pltpu.VMEM((2, members, *piece), bf16),
            pltpu.VMEM((2, members, *piece), bf16),
            pltpu.VMEM((members, 2, dv), f32),
            pltpu.VMEM((groups, 2, dv), f32),
            pltpu.VMEM((8, dv), f32),
            dma((6,)),
            dma((2, members)),
            dma((2, max(head_total, 2))),
            dma((2, 2, members, pieces)),
            dma((2, 2, groups, pieces)),
            dma((2, 2, members, pieces)),
            dma((2, members)),
            dma((2, max(groups, 2))),
            dma((2, max(groups, 2))),
        ],
        compiler_params=pltpu.CompilerParams(
            collective_id=0, has_side_effects=True, vmem_limit_bytes=62 * 2**20
        ),
    )(queries, key_rows, value_rows, log_decay, upstream, norm_gain)
    return pl.pallas_call(
        write_out,
        out_shape=shapes,
        in_specs=[in_vmem] * 5,
        out_specs=(in_hbm,) * 5,
        scratch_shapes=[dma((5,))],
        compiler_params=pltpu.CompilerParams(vmem_limit_bytes=62 * 2**20),
    )(*results)


def solution(mesh):
    in_specs = (
        P("seq", "head"),
        P("seq", "head"),
        P("seq", "head"),
        P("head", "seq"),
        P(("seq", "head"), None),
        P("head", None),
    )
    out_specs = (
        P("seq", "head"),
        P("seq", "head"),
        P("seq", "head"),
        P("head", None),
        P("head", None),
    )
    return jax.shard_map(shards, mesh=mesh, in_specs=in_specs, out_specs=out_specs, check_vma=False)
```

```python
import functools

import jax
import jax.numpy as jnp
from jax import lax
from jax.experimental import pallas as pl
from jax.experimental.pallas import tpu as pltpu
from jax.sharding import PartitionSpec as P

norm_eps = 1e-05
f32, bf16 = jnp.float32, jnp.bfloat16
PIECES = 4


def dot_nn(a, b):
    return lax.dot_general(a, b, (((1,), (0,)), ((), ())), preferred_element_type=f32)


def dot_nt(a, b):
    return lax.dot_general(a, b, (((1,), (1,)), ((), ())), preferred_element_type=f32)


def dot_tn(a, b):
    return lax.dot_general(a, b, (((0,), (0,)), ((), ())), preferred_element_type=f32)


def kernel(
    seq_total, head_total, members, pieces,
    q_hbm, k_hbm, v_hbm, decay_hbm, up_hbm, gain_hbm,
    qg_ref, kg_ref, vg_ref, gg_ref, bg_ref,
    q_ref, k_ref, v_ref, decay_ref, gain_ref, up_ref, total_ref, span_ref,
    turned, lsend, lrecv, carry, csend, psend, state, stat_in, stat_z, stat_sum,
    load_sem, total_sem, up_sem, scatter_sem, chain_sem, spread_sem, stat_sem, statz_sem, span_sem,
):
    me = lax.axis_index("seq")
    head = lax.axis_index("head")
    groups = seq_total // members
    z = me // members
    r = me % members
    rows, dk = q_ref.shape
    dv = v_ref.shape[1]
    scaling = dk ** (-0.5)

    def member(d):
        return lax.rem(r + d, members)

    def remote(src, dst, sems, at, device):
        return pltpu.make_async_remote_copy(
            src_ref=src, dst_ref=dst, send_sem=sems.at[(0, *at)], recv_sem=sems.at[(1, *at)],
            device_id=device, device_id_type=pl.DeviceIdType.MESH,
        )

    def in_group(d):
        return {"seq": z * members + member(d)}

    def other_group(d):
        return {"seq": lax.rem(z + d, groups) * members + r}

    def other_head(d):
        return {"head": lax.rem(head + d, head_total)}

    up_own = up_hbm.at[:, pl.ds(pl.multiple_of(head * dv, dv), dv)]
    loads = [
        pltpu.make_async_copy(src, dst, load_sem.at[i])
        for i, (src, dst) in enumerate((
            (decay_hbm, decay_ref), (k_hbm, k_ref), (v_hbm, v_ref), (q_hbm, q_ref),
            (gain_hbm, gain_ref), (up_own, up_ref.at[head]),
        ))
    ]
    for load in loads:
        load.start()

    barrier = pltpu.get_barrier_semaphore()
    partners = (
        [in_group(d) for d in range(1, members)]
        + [other_group(d) for d in range(1, groups)]
        + [other_head(d) for d in range(1, head_total)]
    )
    for partner in partners:
        pl.semaphore_signal(barrier, inc=1, device_id=partner, device_id_type=pl.DeviceIdType.MESH)

    loads[0].wait()
    decays = decay_ref[...]
    at_row = lax.broadcasted_iota(jnp.int32, (rows, rows), 0)
    at_col = lax.broadcasted_iota(jnp.int32, (rows, rows), 1)
    lower = at_row >= at_col
    running = jnp.sum(jnp.where(lower, decays, 0.0), axis=1, keepdims=True)
    running_row = jnp.sum(jnp.where(at_row == at_col, running, 0.0), axis=0, keepdims=True)
    block_total = running[rows - 1 : rows, :]
    tail_decay = jnp.exp(block_total - running)
    head_decay = jnp.exp(running)
    total_ref[r] = jnp.broadcast_to(block_total, total_ref.shape[1:])
    loads[1].wait()
    loads[2].wait()
    keys, values = k_ref[...], v_ref[...]
    key_decayed = (keys.astype(f32) * tail_decay).astype(bf16)
    turned[0] = key_decayed.T.reshape(turned.shape[1:])

    def scatter_copy(way, d, s):
        return remote(
            lsend.at[way, member(d), s], lrecv.at[way, r, s], scatter_sem, (way, d, s), in_group(d)
        )

    def scatter_arrival(way, d, s):
        return remote(
            lsend.at[way, member(d), s], lrecv.at[way, member(members - d), s], scatter_sem,
            (way, d, s), in_group(d),
        )

    def sends_to(way, d):
        return z + d < groups if way == 0 else z - d >= 0

    def chain_copy(way, d, s):
        return remote(
            csend.at[way, s], carry.at[way, z, s], chain_sem, (way, d, s),
            other_group(d if way == 0 else groups - d),
        )

    def chain_arrival(way, d, s):
        source = lax.rem(z + (groups - d if way == 0 else d), groups)
        return remote(
            csend.at[way, s], carry.at[way, source, s], chain_sem, (way, d, s),
            other_group(d if way == 0 else groups - d),
        )

    def span_copy(d):
        return remote(span_ref.at[z], span_ref.at[z], span_sem, (d,), other_group(d))

    def span_arrival(d):
        slot = span_ref.at[lax.rem(z + groups - d, groups)]
        return remote(slot, slot, span_sem, (d,), other_group(d))

    def spread_copy(way, d, s):
        return remote(
            psend.at[way, member(d), s], state.at[way, r, s], spread_sem, (way, d, s), in_group(d)
        )

    def spread_arrival(way, d, s):
        return remote(
            psend.at[way, member(d), s], state.at[way, member(members - d), s], spread_sem,
            (way, d, s), in_group(d),
        )

    def total_copy(d):
        return remote(total_ref.at[r], total_ref.at[r], total_sem, (d,), in_group(d))

    def total_arrival(d):
        slot = total_ref.at[member(members - d)]
        return remote(slot, slot, total_sem, (d,), in_group(d))

    def up_copy(d):
        whom = lax.rem(head + d, head_total)
        return remote(
            up_hbm.at[:, pl.ds(pl.multiple_of(whom * dv, dv), dv)], up_ref.at[head], up_sem, (d,),
            other_head(d),
        )

    def up_arrival(d):
        whom = lax.rem(head + head_total - d, head_total)
        return remote(up_hbm.at[:, pl.ds(0, dv)], up_ref.at[whom], up_sem, (d,), other_head(d))

    def stat_copy(d):
        return remote(stat_in.at[r], stat_in.at[r], stat_sem, (d,), in_group(d))

    def stat_arrival(d):
        slot = stat_in.at[member(members - d)]
        return remote(slot, slot, stat_sem, (d,), in_group(d))

    def statz_copy(d):
        return remote(stat_z.at[z], stat_z.at[z], statz_sem, (d,), other_group(d))

    def statz_arrival(d):
        slot = stat_z.at[lax.rem(z + groups - d, groups)]
        return remote(slot, slot, statz_sem, (d,), other_group(d))

    def scatter(way, right):
        for d in [members // 2, *(d for d in range(1, members) if d != members // 2), 0]:
            part = dot_nn(turned[way, member(d)], right).astype(bf16).reshape(lsend.shape[2:])
            if d:
                lsend[way, member(d)] = part
                for s in range(pieces):
                    scatter_copy(way, d, s).start()
            else:
                lrecv[way, r] = part

    def chain(way, group_decays):
        order = range(members) if way == 0 else range(members - 1, -1, -1)
        for other in range(groups):

            @pl.when(other >= z if way == 0 else other <= z)
            def _():
                carry[way, other] = jnp.zeros(carry.shape[2:], bf16)

        for s in range(pieces):
            for d in range(1, members):
                scatter_arrival(way, d, s).wait_recv()
            total = None
            for m in order:
                part = lrecv[way, m, s].astype(f32)
                total = part if total is None else group_decays[m] * total + part
            csend[way, s] = total.astype(bf16)
            for d in range(1, groups):

                @pl.when(sends_to(way, d))
                def _():
                    chain_copy(way, d, s).start()

        if way == 0:
            for d in range(1, groups):
                span_arrival(d).wait_recv()
        spans = []
        for other in range(groups):
            ahead = other < z if way == 0 else other > z
            spans.append(jnp.exp(jnp.where(ahead, span_ref[other, 0:1, 0:1], 0.0)))
        for s in range(pieces):
            for d in range(1, groups):

                @pl.when(sends_to(1 - way, d))
                def _():
                    chain_arrival(way, d, s).wait_recv()

            now = jnp.zeros(carry.shape[3:], f32)
            for other in range(groups) if way == 0 else range(groups - 1, -1, -1):
                now = spans[other] * now + carry[way, other, s].astype(f32)
            for at, m in enumerate(order):
                psend[way, m, s] = now.astype(bf16)
                if at < members - 1:
                    now = group_decays[m] * now + lrecv[way, m, s].astype(f32)
            for d in [members // 2, *(d for d in range(1, members) if d != members // 2)]:
                spread_copy(way, d, s).start()
            state[way, r, s] = psend[way, r, s]

    def gathered(way):
        for s in range(pieces):
            for d in range(1, members):
                spread_arrival(way, d, s).wait_recv()
        return state[way].reshape(dk, dv)

    pl.semaphore_wait(barrier, len(partners))
    for d in range(1, members):
        total_copy(d).start()
    scatter(0, values)
    for d in range(1, head_total):
        up_copy(d).start()

    loads[3].wait()
    queries = q_ref[...]
    decay_mat = jnp.where(lower, jnp.exp(jnp.where(lower, running - running_row, 0.0)), 0.0)
    decay_mat = decay_mat * scaling
    weights = (dot_nt(queries, keys) * decay_mat).astype(bf16)
    query_decayed = (queries.astype(f32) * head_decay).astype(bf16)
    turned[1] = (scaling * query_decayed.astype(f32)).astype(bf16).T.reshape(turned.shape[1:])

    for d in range(1, members):
        total_arrival(d).wait_recv()
    group_decays = [jnp.exp(total_ref[m, 0:1, 0:1]) for m in range(members)]
    span = total_ref[0]
    for m in range(1, members):
        span = span + total_ref[m]
    span_ref[z] = span
    for d in range(1, groups):
        span_copy(d).start()
    chain(0, group_decays)

    inner = dot_nn(weights, values)
    loads[4].wait()
    loads[5].wait()
    for d in range(1, head_total):
        up_arrival(d).wait_recv()
    cotangent = up_ref[...].reshape(rows, dv).astype(f32)
    scaled = cotangent * gain_ref[...]
    scaled_mean = jnp.mean(scaled, axis=-1, keepdims=True)

    state_in = gathered(0)
    output = inner + scaling * dot_nn(query_decayed, state_in)
    centered = output - jnp.mean(output, axis=-1, keepdims=True)
    along = jnp.mean(scaled * centered, axis=-1, keepdims=True)
    inverse = lax.rsqrt(jnp.mean(centered * centered, axis=-1, keepdims=True) + norm_eps)
    normed = centered * inverse
    grad_output = (inverse * (scaled - scaled_mean - normed * (along * inverse))).astype(bf16)
    scatter(1, grad_output)

    stat_in[r, 0:1, :] = jnp.sum(cotangent * normed, axis=0, keepdims=True)
    stat_in[r, 1:2, :] = jnp.sum(cotangent, axis=0, keepdims=True)
    for d in range(1, members):
        stat_copy(d).start()
    grad_weights = (dot_nt(grad_output, values) * decay_mat).astype(bf16)
    chain(1, group_decays)

    qg_ref[...] = (
        dot_nn(grad_weights, keys) + (scaling * head_decay) * dot_nt(grad_output, state_in)
    ).astype(bf16)
    key_inner = dot_tn(grad_weights, queries)
    value_inner = dot_tn(weights, grad_output)
    for d in range(1, members):
        stat_arrival(d).wait_recv()
    both = stat_in[0]
    for m in range(1, members):
        both = both + stat_in[m]
    stat_z[z] = both
    for d in range(1, groups):
        statz_copy(d).start()

    state_after = gathered(1)
    kg_ref[...] = (key_inner + tail_decay * dot_nt(values, state_after)).astype(bf16)
    vg_ref[...] = (value_inner + tail_decay * dot_nn(keys, state_after)).astype(bf16)

    for d in range(1, groups):
        statz_arrival(d).wait_recv()
    both = stat_z[0]
    for m in range(1, groups):
        both = both + stat_z[m]
    both = both * ((rows * seq_total) ** (-0.5))
    gg_ref[...] = both[0:1, :]
    bg_ref[...] = both[1:2, :]

    for d in range(1, members):
        total_copy(d).wait_send()
        stat_copy(d).wait_send()
        for way in range(2):
            for s in range(pieces):
                scatter_copy(way, d, s).wait_send()
                spread_copy(way, d, s).wait_send()
    for d in range(1, head_total):
        up_copy(d).wait_send()
    for d in range(1, groups):
        statz_copy(d).wait_send()
        span_copy(d).wait_send()
    for way in range(2):
        for d in range(1, groups):

            @pl.when(sends_to(way, d))
            def _():
                for s in range(pieces):
                    chain_copy(way, d, s).wait_send()


def write_out(*refs):
    *pairs, sems = refs
    half = len(pairs) // 2
    copies = [
        pltpu.make_async_copy(src, dst, sems.at[i])
        for i, (src, dst) in enumerate(zip(pairs[:half], pairs[half:]))
    ]
    for copy in copies:
        copy.start()
    for copy in copies:
        copy.wait()


def shards(queries, key_rows, value_rows, log_decay, upstream, norm_gain):
    seq_total, head_total = lax.axis_size("seq"), lax.axis_size("head")
    members = 4 if seq_total % 4 == 0 else 1
    groups = seq_total // members
    rows, dk = queries.shape
    dv = value_rows.shape[1]
    pieces = PIECES
    piece = (pieces, dk // members // pieces, dv)
    in_hbm = pl.BlockSpec(memory_space=pltpu.HBM)
    in_vmem = pl.BlockSpec(memory_space=pltpu.VMEM)
    shapes = (
        jax.ShapeDtypeStruct((rows, dk), bf16),
        jax.ShapeDtypeStruct((rows, dk), bf16),
        jax.ShapeDtypeStruct((rows, dv), bf16),
        jax.ShapeDtypeStruct((1, dv), f32),
        jax.ShapeDtypeStruct((1, dv), f32),
    )
    dma = pltpu.SemaphoreType.DMA
    results = pl.pallas_call(
        functools.partial(kernel, seq_total, head_total, members, pieces),
        out_shape=shapes,
        in_specs=[in_hbm] * 6,
        out_specs=(in_vmem,) * 5,
        scratch_shapes=[
            pltpu.VMEM((rows, dk), bf16),
            pltpu.VMEM((rows, dk), bf16),
            pltpu.VMEM((rows, dv), bf16),
            pltpu.VMEM((1, rows), f32),
            pltpu.VMEM((1, dv), f32),
            pltpu.VMEM((head_total, rows // head_total, dv), bf16),
            pltpu.VMEM((members, 8, 128), f32),
            pltpu.VMEM((groups, 8, 128), f32),
            pltpu.VMEM((2, members, dk // members, rows), bf16),
            pltpu.VMEM((2, members, *piece), bf16),
            pltpu.VMEM((2, members, *piece), bf16),
            pltpu.VMEM((2, groups, *piece), bf16),
            pltpu.VMEM((2, *piece), bf16),
            pltpu.VMEM((2, members, *piece), bf16),
            pltpu.VMEM((2, members, *piece), bf16),
            pltpu.VMEM((members, 2, dv), f32),
            pltpu.VMEM((groups, 2, dv), f32),
            pltpu.VMEM((8, dv), f32),
            dma((6,)),
            dma((2, members)),
            dma((2, max(head_total, 2))),
            dma((2, 2, members, pieces)),
            dma((2, 2, groups, pieces)),
            dma((2, 2, members, pieces)),
            dma((2, members)),
            dma((2, max(groups, 2))),
            dma((2, max(groups, 2))),
        ],
        compiler_params=pltpu.CompilerParams(
            collective_id=0, has_side_effects=True, vmem_limit_bytes=62 * 2**20
        ),
    )(queries, key_rows, value_rows, log_decay, upstream, norm_gain)
    return pl.pallas_call(
        write_out,
        out_shape=shapes,
        in_specs=[in_vmem] * 5,
        out_specs=(in_hbm,) * 5,
        scratch_shapes=[dma((5,))],
        compiler_params=pltpu.CompilerParams(vmem_limit_bytes=62 * 2**20),
    )(*results)


def solution(mesh):
    in_specs = (
        P("seq", "head"),
        P("seq", "head"),
        P("seq", "head"),
        P("head", "seq"),
        P(("seq", "head"), None),
        P("head", None),
    )
    out_specs = (
        P("seq", "head"),
        P("seq", "head"),
        P("seq", "head"),
        P("head", None),
        P("head", None),
    )
    return jax.shard_map(shards, mesh=mesh, in_specs=in_specs, out_specs=out_specs, check_vma=False)
```
